32 devices in a mesh: dp: 4 (over z), ctx: 8 (over y, x, core).
Axes of the slice: x: 2, y: 2, z: 4, core: 2. Of those that a mesh axis runs over, the one named last changes fastest.
Arguments:
- tokens: int32 [4096], P('ctx'), may hold values from 0 to 4
- queries: bfloat16 [4096, 2048], P('ctx', 'dp'), may hold values from -6 to 6
- keys: bfloat16 [4096, 2048], P('ctx', 'dp'), may hold values from -6 to 6
- values: bfloat16 [4096, 2048], P('ctx', 'dp'), may hold values from -6 to 6
- upstream: bfloat16 [4096, 2048], P('ctx', 'dp'), may hold values from -6 to 6
- filter_taps: float32 [4096, 512], P('ctx'), may hold values from -6 to 6
Outputs:
- conv_out: bfloat16 [4096, 2048], P('ctx', 'dp')
- query_grad: bfloat16 [4096, 2048], P('ctx', 'dp')
- key_grad: bfloat16 [4096, 2048], P('ctx', 'dp')
- value_grad: bfloat16 [4096, 2048], P('ctx', 'dp')
- filter_grad: float32 [4096, 512], P('ctx')
The draws below stay inside these ranges and needn't reach their ends.
Inputs may be any that keep to these rules, and one draw needn't show every extreme that they name: `tokens`: DNA letters: 0 to 3 for A, C, G, T, and 4 for an unknown base, whose positions carry no loss.
All inputs are finite; a program needn't handle non-finite values.
Results may differ from the reference program's by a relative error of at most 0.005.
Values may be sent and summed in bfloat16 or wider, within the bound.
A program may use at most 128 MiB of HBM per device.

```python
import math
import jax
import jax.numpy as jnp
from jax import lax

D = 2048
SEQ = 4096
FILTERS = 512
N_DP = 4


def place_ends(drawn, key, smallest, top_value):
    longest = drawn.shape.index(max(drawn.shape))
    spots = []
    for shift in (0, 1):
        where = [jax.random.randint(jax.random.fold_in(key, axis), (), 0, length) for axis, length in enumerate(drawn.shape)]
        where[longest] = (where[longest] + shift) % drawn.shape[longest]
        spots.append(tuple(where))
    return drawn.at[spots[0]].set(smallest).at[spots[1]].set(top_value)


def block_scale(own_key, dims, shards, low, top_value):
    def one(dim, blocks):
        heights = jax.random.uniform(jax.random.fold_in(jax.random.fold_in(own_key, 6), dim), (blocks,), jnp.float32, low / len(shards), top_value / len(shards))
        return jnp.repeat(jnp.exp(heights), dims[dim] // blocks).reshape((-1,) + (1,) * (len(dims) - dim - 1))

    loudness = one(*shards[0])
    for cut in shards[1:]:
        loudness = loudness * one(*cut)
    return loudness


def centred(stream_key, dims, scale, limit, cuts=(), dtype=jnp.bfloat16):
    values = jax.random.normal(stream_key, dims, jnp.float32) * scale
    if len(cuts) > 0:
        values = block_scale(stream_key, dims, cuts, -0.22, 0.18) * values
    return jnp.clip(values, min=-limit, max=limit).astype(dtype)


def setup_inputs(seed: int = 0) -> dict:
    seeds = jax.random.split(jax.random.key(seed), 7)
    return {
        "tokens": place_ends(jax.random.randint(seeds[0], (SEQ,), 0, 5), jax.random.fold_in(seeds[0], 1), 0, 4).astype(jnp.int32),
        "queries": centred(seeds[1], (SEQ, D), 1.0, 6.0, ((0, 8), (1, 4))),
        "keys": centred(seeds[2], (SEQ, D), 1.0, 6.0, ((0, 8), (1, 4))),
        "values": centred(seeds[3], (SEQ, D), 1.0, 6.0, ((0, 8), (1, 4))),
        "upstream": centred(seeds[4], (SEQ, D), 1.0, 6.0, ((0, 8), (1, 4))),
        "filter_taps": centred(seeds[5], (SEQ, FILTERS), 1.0, 6.0, ((0, 8),), jnp.float32),
    }


def reference(tokens, queries, keys, values, upstream, filter_taps):
    length = 2 * SEQ
    scale = 1.0 / math.sqrt(SEQ)
    keep = (tokens != 4).astype(jnp.float32)[:, None]
    taps = filter_taps.astype(jnp.float32) * scale
    spec_h = jnp.fft.fft(taps, n=length, axis=0)

    def grouped(array):
        return array.reshape(SEQ, N_DP, FILTERS).transpose(1, 0, 2)

    def one_group(items):
        query_row, key_row, value_row, grad_row = items
        grad_in = grad_row.astype(jnp.float32) * keep
        query32 = query_row.astype(jnp.float32)
        key32 = key_row.astype(jnp.float32)
        value32 = value_row.astype(jnp.float32)
        gated = lax.optimization_barrier((key32 * value32).astype(jnp.bfloat16))
        into = lax.optimization_barrier((grad_in * query32).astype(jnp.bfloat16))
        spec_u = jnp.fft.fft(gated.astype(jnp.float32), n=length, axis=0)
        spec_dz = jnp.fft.fft(into.astype(jnp.float32), n=length, axis=0)
        conv = jnp.real(jnp.fft.ifft(spec_h * spec_u, axis=0))[:SEQ]
        back = jnp.real(jnp.fft.ifft(jnp.conj(spec_h) * spec_dz, axis=0))[:SEQ]
        corr = jnp.real(jnp.fft.ifft(jnp.conj(spec_u) * spec_dz, axis=0))[:SEQ]
        return ((query32 * conv).astype(jnp.bfloat16), (grad_in * conv).astype(jnp.bfloat16), (back * value32).astype(jnp.bfloat16), (back * key32).astype(jnp.bfloat16), corr)
    results = lax.map(one_group, (grouped(queries), grouped(keys), grouped(values), grouped(upstream)))

    def joined(array):
        return array.transpose(1, 0, 2).reshape(SEQ, D)
    filter_grad = (lax.optimization_barrier(jnp.sum(results[4], axis=0)) * scale).astype(jnp.float32)
    return (joined(results[0]), joined(results[1]), joined(results[2]), joined(results[3]), filter_grad)
```

```python
import math

import jax
import jax.numpy as jnp
import ml_dtypes
import numpy as np
from jax import lax
from jax.experimental import pallas as pl
from jax.experimental.pallas import tpu as pltpu
from jax.sharding import PartitionSpec as P

two_pi = 2.0 * math.pi
TILE = 16


def rotate(count, modulus):
    angle = -two_pi / modulus * (count % modulus).astype(jnp.float32)
    return (jnp.cos(angle), jnp.sin(angle))


def contract(form, table, data):
    return jnp.einsum(form, table, data, precision=lax.Precision.HIGHEST)


def ahead_outer(signal, start, length):
    width = signal.shape[1]
    places = start + jnp.arange(signal.shape[2], dtype=jnp.int32)
    kfreq = jnp.arange(2 * width, dtype=jnp.int32)
    cosine, sine = rotate(kfreq[:, None] * jnp.arange(width, dtype=jnp.int32)[None, :], 2 * width)
    real_part = contract("kp,sprc->skrc", cosine, signal)
    imag_part = contract("kp,sprc->skrc", sine, signal)
    twist_c, twist_s = rotate(kfreq[:, None] * places[None, :], length)
    twist_c = twist_c[None, :, :, None]
    twist_s = twist_s[None, :, :, None]
    return jnp.stack(
        [real_part * twist_c - imag_part * twist_s, real_part * twist_s + imag_part * twist_c]
    )


def ahead_inner(spectrum):
    index = jnp.arange(spectrum.shape[3], dtype=jnp.int32)
    cosine, sine = rotate(index[:, None] * index[None, :], spectrum.shape[3])
    real_part = contract("ji,skic->skjc", cosine, spectrum[0]) - contract(
        "ji,skic->skjc", sine, spectrum[1]
    )
    imag_part = contract("ji,skic->skjc", cosine, spectrum[1]) + contract(
        "ji,skic->skjc", sine, spectrum[0]
    )
    return jnp.stack([real_part, imag_part])


def back_inner(spectrum, kstart, length):
    index = jnp.arange(spectrum.shape[3], dtype=jnp.int32)
    cosine, sine = rotate(index[:, None] * index[None, :], spectrum.shape[3])
    real_part = contract("ji,skjc->skic", cosine, spectrum[0]) + contract(
        "ji,skjc->skic", sine, spectrum[1]
    )
    imag_part = contract("ji,skjc->skic", cosine, spectrum[1]) - contract(
        "ji,skjc->skic", sine, spectrum[0]
    )
    kfreq = kstart + jnp.arange(spectrum.shape[2], dtype=jnp.int32)
    twist_c, twist_s = rotate(kfreq[:, None] * index[None, :], length)
    twist_c = twist_c[None, :, :, None]
    twist_s = twist_s[None, :, :, None]
    return jnp.stack(
        [real_part * twist_c + imag_part * twist_s, imag_part * twist_c - real_part * twist_s]
    )


def back_outer(spectrum, length):
    width = spectrum.shape[2] // 2
    kfreq = jnp.arange(2 * width, dtype=jnp.int32)
    cosine, sine = rotate(kfreq[:, None] * jnp.arange(width, dtype=jnp.int32)[None, :], 2 * width)
    total = contract("kp,skrc->sprc", cosine, spectrum[0]) + contract(
        "kp,skrc->sprc", sine, spectrum[1]
    )
    return total / length


def spectral_terms(spectra):
    u_real, u_imag = (spectra[0, 0], spectra[1, 0])
    z_real, z_imag = (spectra[0, 1], spectra[1, 1])
    filt_r, filt_i = (spectra[0, 2], spectra[1, 2])
    forward_real = filt_r * u_real - filt_i * u_imag
    forward_imag = filt_r * u_imag + filt_i * u_real
    backward_real = filt_r * z_real + filt_i * z_imag
    backward_imag = filt_r * z_imag - filt_i * z_real
    corr_real = u_real * z_real + u_imag * z_imag
    corr_imag = u_real * z_imag - u_imag * z_real
    return jnp.stack(
        [
            jnp.stack([forward_real, backward_real, corr_real]),
            jnp.stack([forward_imag, backward_imag, corr_imag]),
        ]
    )


def on_device(tokens, queries, keys, values, upstream, filter_taps):
    rows = queries.shape[0]
    parts = lax.axis_size("ctx")
    length = 2 * rows * parts
    scale = 1.0 / math.sqrt(rows * parts)
    keep = (tokens != 4).astype(jnp.float32)[:, None]
    grad_in = upstream.astype(jnp.float32) * keep
    query32 = queries.astype(jnp.float32)
    key32 = keys.astype(jnp.float32)
    value32 = values.astype(jnp.float32)
    gated = (key32 * value32).astype(jnp.bfloat16)
    into = (grad_in * query32).astype(jnp.bfloat16)
    paired = jnp.stack([gated, into])
    taps = filter_taps * scale
    sliver = rows // parts
    moved = lax.all_to_all(paired[:, None], "ctx", split_axis=2, concat_axis=1, tiled=True)
    moved_taps = lax.all_to_all(taps[None, None], "ctx", split_axis=2, concat_axis=1, tiled=True)
    signal = jnp.concatenate([moved.astype(jnp.float32), moved_taps], axis=0)
    first = ahead_outer(signal, lax.axis_index("ctx") * sliver, length)
    turned = lax.all_to_all(first, "ctx", split_axis=2, concat_axis=3, tiled=True)
    products = spectral_terms(ahead_inner(turned))
    inner = back_inner(products, 2 * lax.axis_index("ctx"), length)
    spread = lax.all_to_all(inner, "ctx", split_axis=3, concat_axis=2, tiled=True)
    outer = back_outer(spread, length)
    fields = lax.all_to_all(outer, "ctx", split_axis=1, concat_axis=2, tiled=True)[:, 0]
    filter_grad = lax.psum(fields[2], "dp") * scale
    conv = fields[0]
    back = fields[1]
    conv_out = (query32 * conv).astype(jnp.bfloat16)
    query_grad = (grad_in * conv).astype(jnp.bfloat16)
    key_grad = (back * value32).astype(jnp.bfloat16)
    value_grad = (back * key32).astype(jnp.bfloat16)
    return (conv_out, query_grad, key_grad, value_grad, filter_grad)


def split(table):
    high = table.astype(ml_dtypes.bfloat16)
    low = (table - high.astype(np.float64)).astype(ml_dtypes.bfloat16)
    return (high, low)


def tables():
    p = np.arange(32)
    rows = [np.ones(32), np.cos(np.pi * p)]
    weight = [1.0, 1.0]
    for k in range(1, 32):
        rows.append(np.cos(2 * np.pi * k * p / 64))
        rows.append(-np.sin(2 * np.pi * k * p / 64))
        weight += [2.0, 2.0]
    lead = np.stack(rows)
    eye = np.eye(TILE)
    ahead = np.concatenate(split(np.kron(lead, eye)), axis=1)
    behind = lead.T * np.array(weight)[None, :] / 8192.0
    behind = np.concatenate(split(np.kron(behind, eye)), axis=1)
    angle = 2 * np.pi * np.outer(np.arange(128), np.arange(128)) / 128
    cosine, sine = np.cos(angle), np.sin(angle)
    inner = np.block([[cosine, sine], [-sine, cosine]])
    inner_ahead = np.stack(split(inner))
    inner_behind = np.stack(split(inner.T))
    twist = 2 * np.pi * np.outer(np.arange(33), np.arange(128)) / 8192
    twist = np.stack([np.cos(twist), -np.sin(twist)], axis=1).astype(np.float32)
    twist = np.ascontiguousarray(np.broadcast_to(twist[..., None], (33, 2, 128, 128)))
    return (ahead, behind, inner_ahead, inner_behind, twist)


def dot(left, right):
    return jnp.dot(left, right, preferred_element_type=jnp.float32)


def dot_split(table_ref, data):
    high = data.astype(jnp.bfloat16)
    low = (data - high.astype(jnp.float32)).astype(jnp.bfloat16)
    return dot(table_ref[0], high) + dot(table_ref[0], low) + dot(table_ref[1], high)


def transform(z_ref, h_ref, tabs, a_ref, s_ref, emit):
    ahead, behind, inner_ahead, inner_behind, twist = tabs
    chunk = 8

    def first(step, _):
        places = pl.ds(pl.multiple_of(step * TILE, TILE), TILE)
        data = jnp.concatenate(
            [z_ref[:, places, :].reshape(32 * TILE, 128), h_ref[:, places, :].reshape(32 * TILE, 128)],
            axis=1,
        )
        for part in range(64 // chunk):
            lines = slice(part * chunk * TILE, (part + 1) * chunk * TILE)
            out = dot(ahead[lines, : 32 * TILE], data) + dot(ahead[lines, 32 * TILE :], data)
            a_ref[part * chunk : (part + 1) * chunk, places, :] = out.reshape(chunk, TILE, 256)
        return 0

    lax.fori_loop(0, 128 // TILE, first, 0)

    lane = lax.broadcasted_iota(jnp.int32, (128, 128), 1)
    sign = jnp.where(lane < 64, 1.0, -1.0)

    def middle(k, real_part, imag_part):
        cosine, sine = twist[k, 0], twist[k, 1]
        halves = []
        for side in (0, 128):
            re = real_part[:, side : side + 128]
            if imag_part is None:
                halves.append((re * cosine, re * sine))
            else:
                im = imag_part[:, side : side + 128]
                halves.append((re * cosine - im * sine, re * sine + im * cosine))
        data = jnp.concatenate(
            [jnp.concatenate([halves[0][0], halves[1][0]], axis=1),
             jnp.concatenate([halves[0][1], halves[1][1]], axis=1)], axis=0)
        spec = dot_split(inner_ahead, data)
        ur, ui = spec[:128, :128], spec[128:, :128]
        hr, hi = spec[:128, 128:], spec[128:, 128:] * sign
        zr, zi = pltpu.roll(ur, 64, 1), pltpu.roll(ui, 64, 1)
        real_part = jnp.concatenate([hr * ur - hi * ui, ur * zr + ui * zi], axis=1)
        imag_part = jnp.concatenate([hr * ui + hi * ur, ur * zi - ui * zr], axis=1)
        time = dot_split(inner_behind, jnp.concatenate([real_part, imag_part], axis=0))
        outs = []
        for side in (0, 128):
            re, im = time[:128, side : side + 128], time[128:, side : side + 128]
            outs.append((re * cosine + im * sine, im * cosine - re * sine))
        return (
            jnp.concatenate([outs[0][0], outs[1][0]], axis=1).astype(jnp.bfloat16),
            jnp.concatenate([outs[0][1], outs[1][1]], axis=1).astype(jnp.bfloat16),
        )

    s_ref[0] = middle(0, a_ref[0], None)[0]
    s_ref[1] = middle(32, a_ref[1], None)[0]

    def second(k, _):
        real_part, imag_part = middle(k, a_ref[2 * k], a_ref[2 * k + 1])
        s_ref[2 * k] = real_part
        s_ref[2 * k + 1] = imag_part
        return 0

    lax.fori_loop(1, 32, second, 0)

    def last(step, _):
        places = pl.ds(pl.multiple_of(step * TILE, TILE), TILE)
        data = s_ref[:, places, :].reshape(64 * TILE, 256)
        for part in range(32 // chunk):
            lines = slice(part * chunk * TILE, (part + 1) * chunk * TILE)
            out = dot(behind[lines, : 64 * TILE], data) + dot(behind[lines, 64 * TILE :], data)
            emit(part * chunk, chunk, places, out.reshape(chunk, TILE, 256))
        return 0

    lax.fori_loop(0, 128 // TILE, last, 0)


def local_kernel(z_ref, h_ref, *refs):
    tabs, (pair_ref, corr_ref, a_ref, s_ref) = refs[:5], refs[5:]

    def emit(start, count, places, out):
        pair_ref[start : start + count, places, :] = out[:, :, :128].astype(jnp.bfloat16)
        corr_ref[start : start + count, places, :] = out[:, :, 128:].astype(jnp.bfloat16)

    transform(z_ref, h_ref, tabs, a_ref, s_ref, emit)


def local_convolution(paired, taps):
    tabs = [jnp.asarray(t) for t in tables()]
    whole = pl.BlockSpec(memory_space=pltpu.VMEM)
    shape = jax.ShapeDtypeStruct((32, 128, 128), jnp.bfloat16)
    return pl.pallas_call(
        local_kernel,
        out_shape=(shape, shape),
        in_specs=[whole] * 7,
        out_specs=(whole, whole),
        scratch_shapes=[pltpu.VMEM((64, 128, 256), jnp.float32), pltpu.VMEM((64, 128, 256), jnp.bfloat16)],
        compiler_params=pltpu.CompilerParams(vmem_limit_bytes=48 * 1024 * 1024),
    )(paired, taps, *tabs)


def by_channel(tokens, queries, keys, values, upstream, filter_taps):
    rows = queries.shape[0]
    scale = 1.0 / 64.0
    keep = (tokens != 4).astype(jnp.float32)[:, None]
    grad_in = upstream.astype(jnp.float32) * keep
    query32 = queries.astype(jnp.float32)
    key32 = keys.astype(jnp.float32)
    value32 = values.astype(jnp.float32)
    gated = (key32 * value32).astype(jnp.bfloat16)
    into = (grad_in * query32).astype(jnp.bfloat16)
    taps = (filter_taps * scale).astype(jnp.bfloat16)
    cut = lambda array: array.reshape(rows, 8, 64).transpose(1, 0, 2)
    paired = jnp.concatenate([cut(gated), cut(into)], axis=2)
    taps = cut(taps)
    paired = lax.all_to_all(paired, "ctx", split_axis=0, concat_axis=0, tiled=True)
    taps = lax.all_to_all(taps, "ctx", split_axis=0, concat_axis=0, tiled=True)
    taps = jnp.concatenate([taps, taps], axis=2)
    pair, corr = local_convolution(paired.reshape(32, 128, 128), taps.reshape(32, 128, 128))
    pair = lax.all_to_all(pair.reshape(8, rows, 128), "ctx", split_axis=0, concat_axis=0, tiled=True)
    corr = corr.reshape(8, rows, 128)[:, :, :64]
    corr = lax.all_to_all(corr, "ctx", split_axis=0, concat_axis=0, tiled=True)
    join = lambda array: array.transpose(1, 0, 2).reshape(rows, 512).astype(jnp.float32)
    conv, back = join(pair[:, :, :64]), join(pair[:, :, 64:])
    filter_grad = lax.psum(join(corr), "dp") * scale
    conv_out = (query32 * conv).astype(jnp.bfloat16)
    query_grad = (grad_in * conv).astype(jnp.bfloat16)
    key_grad = (back * value32).astype(jnp.bfloat16)
    value_grad = (back * key32).astype(jnp.bfloat16)
    return (conv_out, query_grad, key_grad, value_grad, filter_grad)


def either(*args):
    parts = lax.axis_size("ctx")
    fits = parts == 8 and args[1].shape == (512, 512) and args[5].shape == (512, 512)
    return by_channel(*args) if fits else on_device(*args)


def solution(mesh):
    placed = (
        P("ctx"),
        P("ctx", "dp"),
        P("ctx", "dp"),
        P("ctx", "dp"),
        P("ctx", "dp"),
        P("ctx", None),
    )
    return jax.shard_map(
        either,
        mesh=mesh,
        in_specs=placed,
        out_specs=(P("ctx", "dp"), P("ctx", "dp"), P("ctx", "dp"), P("ctx", "dp"), P("ctx", None)),
        check_vma=False,
    )
```

```python
import math

import jax
import jax.numpy as jnp
import ml_dtypes
import numpy as np
from jax import lax
from jax.experimental import pallas as pl
from jax.experimental.pallas import tpu as pltpu
from jax.sharding import PartitionSpec as P

two_pi = 2.0 * math.pi
TILE = 16
MESH = pl.DeviceIdType.MESH


def rotate(count, modulus):
    angle = -two_pi / modulus * (count % modulus).astype(jnp.float32)
    return (jnp.cos(angle), jnp.sin(angle))


def contract(form, table, data):
    return jnp.einsum(form, table, data, precision=lax.Precision.HIGHEST)


def ahead_outer(signal, start, length):
    width = signal.shape[1]
    places = start + jnp.arange(signal.shape[2], dtype=jnp.int32)
    kfreq = jnp.arange(2 * width, dtype=jnp.int32)
    cosine, sine = rotate(kfreq[:, None] * jnp.arange(width, dtype=jnp.int32)[None, :], 2 * width)
    real_part = contract("kp,sprc->skrc", cosine, signal)
    imag_part = contract("kp,sprc->skrc", sine, signal)
    twist_c, twist_s = rotate(kfreq[:, None] * places[None, :], length)
    twist_c = twist_c[None, :, :, None]
    twist_s = twist_s[None, :, :, None]
    return jnp.stack(
        [real_part * twist_c - imag_part * twist_s, real_part * twist_s + imag_part * twist_c]
    )


def ahead_inner(spectrum):
    index = jnp.arange(spectrum.shape[3], dtype=jnp.int32)
    cosine, sine = rotate(index[:, None] * index[None, :], spectrum.shape[3])
    real_part = contract("ji,skic->skjc", cosine, spectrum[0]) - contract(
        "ji,skic->skjc", sine, spectrum[1]
    )
    imag_part = contract("ji,skic->skjc", cosine, spectrum[1]) + contract(
        "ji,skic->skjc", sine, spectrum[0]
    )
    return jnp.stack([real_part, imag_part])


def back_inner(spectrum, kstart, length):
    index = jnp.arange(spectrum.shape[3], dtype=jnp.int32)
    cosine, sine = rotate(index[:, None] * index[None, :], spectrum.shape[3])
    real_part = contract("ji,skjc->skic", cosine, spectrum[0]) + contract(
        "ji,skjc->skic", sine, spectrum[1]
    )
    imag_part = contract("ji,skjc->skic", cosine, spectrum[1]) - contract(
        "ji,skjc->skic", sine, spectrum[0]
    )
    kfreq = kstart + jnp.arange(spectrum.shape[2], dtype=jnp.int32)
    twist_c, twist_s = rotate(kfreq[:, None] * index[None, :], length)
    twist_c = twist_c[None, :, :, None]
    twist_s = twist_s[None, :, :, None]
    return jnp.stack(
        [real_part * twist_c + imag_part * twist_s, imag_part * twist_c - real_part * twist_s]
    )


def back_outer(spectrum, length):
    width = spectrum.shape[2] // 2
    kfreq = jnp.arange(2 * width, dtype=jnp.int32)
    cosine, sine = rotate(kfreq[:, None] * jnp.arange(width, dtype=jnp.int32)[None, :], 2 * width)
    total = contract("kp,skrc->sprc", cosine, spectrum[0]) + contract(
        "kp,skrc->sprc", sine, spectrum[1]
    )
    return total / length


def spectral_terms(spectra):
    u_real, u_imag = (spectra[0, 0], spectra[1, 0])
    z_real, z_imag = (spectra[0, 1], spectra[1, 1])
    filt_r, filt_i = (spectra[0, 2], spectra[1, 2])
    forward_real = filt_r * u_real - filt_i * u_imag
    forward_imag = filt_r * u_imag + filt_i * u_real
    backward_real = filt_r * z_real + filt_i * z_imag
    backward_imag = filt_r * z_imag - filt_i * z_real
    corr_real = u_real * z_real + u_imag * z_imag
    corr_imag = u_real * z_imag - u_imag * z_real
    return jnp.stack(
        [
            jnp.stack([forward_real, backward_real, corr_real]),
            jnp.stack([forward_imag, backward_imag, corr_imag]),
        ]
    )


def on_device(tokens, queries, keys, values, upstream, filter_taps):
    rows = queries.shape[0]
    parts = lax.axis_size("ctx")
    length = 2 * rows * parts
    scale = 1.0 / math.sqrt(rows * parts)
    keep = (tokens != 4).astype(jnp.float32)[:, None]
    grad_in = upstream.astype(jnp.float32) * keep
    query32 = queries.astype(jnp.float32)
    key32 = keys.astype(jnp.float32)
    value32 = values.astype(jnp.float32)
    gated = (key32 * value32).astype(jnp.bfloat16)
    into = (grad_in * query32).astype(jnp.bfloat16)
    paired = jnp.stack([gated, into])
    taps = filter_taps * scale
    sliver = rows // parts
    moved = lax.all_to_all(paired[:, None], "ctx", split_axis=2, concat_axis=1, tiled=True)
    moved_taps = lax.all_to_all(taps[None, None], "ctx", split_axis=2, concat_axis=1, tiled=True)
    signal = jnp.concatenate([moved.astype(jnp.float32), moved_taps], axis=0)
    first = ahead_outer(signal, lax.axis_index("ctx") * sliver, length)
    turned = lax.all_to_all(first, "ctx", split_axis=2, concat_axis=3, tiled=True)
    products = spectral_terms(ahead_inner(turned))
    inner = back_inner(products, 2 * lax.axis_index("ctx"), length)
    spread = lax.all_to_all(inner, "ctx", split_axis=3, concat_axis=2, tiled=True)
    outer = back_outer(spread, length)
    fields = lax.all_to_all(outer, "ctx", split_axis=1, concat_axis=2, tiled=True)[:, 0]
    filter_grad = lax.psum(fields[2], "dp") * scale
    conv = fields[0]
    back = fields[1]
    conv_out = (query32 * conv).astype(jnp.bfloat16)
    query_grad = (grad_in * conv).astype(jnp.bfloat16)
    key_grad = (back * value32).astype(jnp.bfloat16)
    value_grad = (back * key32).astype(jnp.bfloat16)
    return (conv_out, query_grad, key_grad, value_grad, filter_grad)


def split(table):
    high = table.astype(ml_dtypes.bfloat16)
    low = (table - high.astype(np.float64)).astype(ml_dtypes.bfloat16)
    return (high, low)


def tables():
    p = np.arange(32)
    rows = [np.ones(32), np.cos(np.pi * p)]
    weight = [1.0, 1.0]
    for k in range(1, 32):
        rows.append(np.cos(2 * np.pi * k * p / 64))
        rows.append(-np.sin(2 * np.pi * k * p / 64))
        weight += [2.0, 2.0]
    lead = np.stack(rows)
    eye = np.eye(TILE)
    ahead = np.concatenate(split(np.kron(lead, eye)), axis=1)
    behind = lead.T * np.array(weight)[None, :] / 8192.0
    behind = np.concatenate(split(np.kron(behind, eye)), axis=1)
    angle = 2 * np.pi * np.outer(np.arange(128), np.arange(128)) / 128
    cosine, sine = np.cos(angle), np.sin(angle)
    inner = np.block([[cosine, sine], [-sine, cosine]])
    inner_ahead = np.stack(split(inner))
    inner_behind = np.stack(split(inner.T))
    twist = 2 * np.pi * np.outer(np.arange(33), np.arange(128)) / 8192
    twist = np.stack([np.cos(twist), -np.sin(twist)], axis=1).astype(np.float32)
    twist = np.ascontiguousarray(np.broadcast_to(twist[..., None], (33, 2, 128, 128)))
    return (ahead, behind, inner_ahead, inner_behind, twist)


def dot(left, right):
    return jnp.dot(left, right, preferred_element_type=jnp.float32)


def dot_split(table_ref, data):
    high = data.astype(jnp.bfloat16)
    low = (data - high.astype(jnp.float32)).astype(jnp.bfloat16)
    return dot(table_ref[0], high) + dot(table_ref[0], low) + dot(table_ref[1], high)


def transform(z_ref, h_ref, tabs, a_ref, s_ref):
    ahead, behind, inner_ahead, inner_behind, twist = tabs
    chunk = 8

    def first(step, _):
        places = pl.ds(pl.multiple_of(step * TILE, TILE), TILE)
        data = jnp.concatenate(
            [z_ref[:, places, :].reshape(32 * TILE, 128), h_ref[:, places, :].reshape(32 * TILE, 128)],
            axis=1,
        )
        for part in range(64 // chunk):
            lines = slice(part * chunk * TILE, (part + 1) * chunk * TILE)
            out = dot(ahead[lines, : 32 * TILE], data) + dot(ahead[lines, 32 * TILE :], data)
            a_ref[part * chunk : (part + 1) * chunk, places, :] = out.reshape(chunk, TILE, 256)
        return 0

    lax.fori_loop(0, 128 // TILE, first, 0)

    lane = lax.broadcasted_iota(jnp.int32, (128, 128), 1)
    sign = jnp.where(lane < 64, 1.0, -1.0)

    def middle(k, real_part, imag_part):
        cosine, sine = twist[k, 0], twist[k, 1]
        halves = []
        for side in (0, 128):
            re = real_part[:, side : side + 128]
            if imag_part is None:
                halves.append((re * cosine, re * sine))
            else:
                im = imag_part[:, side : side + 128]
                halves.append((re * cosine - im * sine, re * sine + im * cosine))
        data = jnp.concatenate(
            [jnp.concatenate([halves[0][0], halves[1][0]], axis=1),
             jnp.concatenate([halves[0][1], halves[1][1]], axis=1)], axis=0)
        spec = dot_split(inner_ahead, data)
        ur, ui = spec[:128, :128], spec[128:, :128]
        hr, hi = spec[:128, 128:], spec[128:, 128:] * sign
        zr, zi = pltpu.roll(ur, 64, 1), pltpu.roll(ui, 64, 1)
        real_part = jnp.concatenate([hr * ur - hi * ui, ur * zr + ui * zi], axis=1)
        imag_part = jnp.concatenate([hr * ui + hi * ur, ur * zi - ui * zr], axis=1)
        time = dot_split(inner_behind, jnp.concatenate([real_part, imag_part], axis=0))
        outs = []
        for side in (0, 128):
            re, im = time[:128, side : side + 128], time[128:, side : side + 128]
            outs.append((re * cosine + im * sine, im * cosine - re * sine))
        return (
            jnp.concatenate([outs[0][0], outs[1][0]], axis=1).astype(jnp.bfloat16),
            jnp.concatenate([outs[0][1], outs[1][1]], axis=1).astype(jnp.bfloat16),
        )

    s_ref[0] = middle(0, a_ref[0], None)[0]
    s_ref[1] = middle(32, a_ref[1], None)[0]

    def second(k, _):
        real_part, imag_part = middle(k, a_ref[2 * k], a_ref[2 * k + 1])
        s_ref[2 * k] = real_part
        s_ref[2 * k + 1] = imag_part
        return 0

    lax.fori_loop(1, 32, second, 0, unroll=2)


def low_half(shape):
    return lax.broadcasted_iota(jnp.int32, shape, len(shape) - 1) < 64


def swap(array):
    return pltpu.roll(array, 64, array.ndim - 1)


def block(ref, index):
    return ref.at[pl.ds(4 * index, 4)]


def whole_kernel(
    keep_ref, q_ref, k_ref, v_ref, up_ref, taps_ref,
    ahead, behind, inner_ahead, inner_behind, twist,
    conv_out, query_grad, key_grad, value_grad, filter_grad,
    zs, z_ref, ts, tr, h_ref, a_ref, s_ref, ps, pr, cs, cr, ct, fr, fg,
    z_sems, t_sems, p_sems, c_sems, f_sems, g_sems,
):
    me = lax.axis_index("ctx")
    row = lax.axis_index("dp")
    f32, bf16 = jnp.float32, jnp.bfloat16

    barrier = pltpu.get_barrier_semaphore()
    for step in range(1, 8):
        pl.semaphore_signal(barrier, 1, device_id={"ctx": lax.rem(me + step, 8)}, device_id_type=MESH)
    for step in range(1, 4):
        pl.semaphore_signal(barrier, 1, device_id={"dp": lax.rem(row + step, 4)}, device_id_type=MESH)

    low = low_half((512, 128))
    for pair in range(4):
        cols = slice(128 * pair, 128 * pair + 128)
        gated = k_ref[:, cols].astype(f32) * v_ref[:, cols].astype(f32)
        into = up_ref[:, cols].astype(f32) * keep_ref[...] * q_ref[:, cols].astype(f32)
        zs[8 * pair : 8 * pair + 4] = jnp.where(low, gated, swap(into)).astype(bf16).reshape(4, 128, 128)
        zs[8 * pair + 4 : 8 * pair + 8] = jnp.where(low, swap(gated), into).astype(bf16).reshape(4, 128, 128)
        taps = taps_ref[:, cols] * (1.0 / 64.0)
        top, bottom = taps[:256], taps[256:]
        ts[2 * pair] = jnp.where(low[:256], top, swap(bottom)).astype(bf16)
        ts[2 * pair + 1] = jnp.where(low[:256], swap(top), bottom).astype(bf16)

    pl.semaphore_wait(barrier, 10)

    def to_ctx(source, target, sems, step, peer):
        return pltpu.make_async_remote_copy(
            source, target, sems.at[0, step], sems.at[1, step],
            device_id={"ctx": peer}, device_id_type=MESH)

    def to_dp(source, target, sems, step):
        return pltpu.make_async_remote_copy(
            source, target, sems.at[0, step], sems.at[1, step],
            device_id={"dp": lax.rem(row + step, 4)}, device_id_type=MESH)

    moves = []
    for step in range(1, 8):
        peer = lax.rem(me + step, 8)
        moves.append(to_ctx(block(zs, peer), block(z_ref, me), z_sems, step, peer))
        moves.append(to_ctx(ts.at[peer], tr.at[me], t_sems, step, peer))
    for move in moves:
        move.start()
    z_ref[pl.ds(4 * me, 4)] = zs[pl.ds(4 * me, 4)]
    tr[me] = ts[me]
    for move in moves:
        move.wait()

    def unpack(source, _):
        packed = tr[source].astype(f32)
        turned = swap(packed)
        half = low_half((256, 128))
        h_ref[pl.ds(4 * source, 2)] = jnp.where(half, packed, turned).astype(bf16).reshape(2, 128, 128)
        h_ref[pl.ds(4 * source + 2, 2)] = jnp.where(half, turned, packed).astype(bf16).reshape(2, 128, 128)
        return 0

    lax.fori_loop(0, 8, unpack, 0)
    transform(z_ref, h_ref, (ahead, behind, inner_ahead, inner_behind, twist), a_ref, s_ref)

    def correlate(step, _):
        places = pl.ds(pl.multiple_of(step * TILE, TILE), TILE)
        data = s_ref[:, places, 128:].reshape(64 * TILE, 128)
        half = low_half((4, TILE, 128))
        for part in range(4):
            out = dot(behind[128 * part : 128 * part + 128, : 64 * TILE], data).reshape(8, TILE, 128)
            cs[:, part, places, :] = jnp.where(half, out[:4], swap(out[4:])).astype(bf16)
        return 0

    lax.fori_loop(0, 128 // TILE, correlate, 0)
    summed = [to_dp(cs.at[lax.rem(row + step, 4)], cr.at[step], c_sems, step) for step in range(1, 4)]
    for move in summed:
        move.start()

    returned = []
    for turn in range(1, 5):
        part = lax.rem(me // 2 + turn, 4)

        def convolve(step, _):
            places = pl.ds(pl.multiple_of(step * TILE, TILE), TILE)
            data = s_ref[:, places, :128].reshape(64 * TILE, 128)
            lines = pl.ds(pl.multiple_of(128 * part, 128), 128)
            out = dot(behind[lines, : 64 * TILE], data) + dot(behind[lines, 64 * TILE :], data)
            ps[pl.ds(8 * part, 8), places, :] = out.reshape(8, TILE, 128).astype(bf16)
            return 0

        lax.fori_loop(0, 128 // TILE, convolve, 0)
        peers = [lax.rem(me + 2 * turn, 8), (me // 2 + turn) % 4 * 2 + 1 - me % 2]
        for side, peer in enumerate(peers):
            if turn == 4 and side == 0:
                continue
            move = to_ctx(block(ps, peer), block(pr, me), p_sems, 2 * turn - 2 + side, peer)
            move.start()
            returned.append(move)
    pr[pl.ds(4 * me, 4)] = ps[pl.ds(4 * me, 4)]

    for move in summed:
        move.wait()
    total = cs[row].astype(f32)
    for step in range(1, 4):
        total = total + cr[step].astype(f32)
    ct[...] = total.astype(bf16)
    spread = []
    for step in range(1, 8):
        peer = lax.rem(me + step, 8)
        move = to_ctx(ct.at[peer // 2], fr.at[me], f_sems, step, peer)
        move.start()
        spread.append(move)
    fr[me] = ct[me // 2]
    for move in spread:
        move.wait()
    odd = lax.rem(me, 2)
    half = low_half((128, 128))
    for pair in range(4):
        first, second = fr[2 * pair].astype(f32), fr[2 * pair + 1].astype(f32)
        even_case = jnp.where(half, first, swap(second))
        odd_case = jnp.where(half, swap(first), second)
        fg[row, :, 128 * pair : 128 * pair + 128] = jnp.where(odd == 0, even_case, odd_case).astype(bf16)
    gathered = [to_dp(fg.at[row], fg.at[row], g_sems, step) for step in range(1, 4)]
    for move in gathered:
        move.start()

    for move in returned:
        move.wait()
    for pair in range(4):
        cols = slice(128 * pair, 128 * pair + 128)
        first = pr[8 * pair : 8 * pair + 4].reshape(512, 128).astype(f32)
        second = pr[8 * pair + 4 : 8 * pair + 8].reshape(512, 128).astype(f32)
        conv = jnp.where(low, first, swap(second))
        back = jnp.where(low, swap(first), second)
        conv_out[:, cols] = (q_ref[:, cols].astype(f32) * conv).astype(bf16)
        query_grad[:, cols] = (up_ref[:, cols].astype(f32) * keep_ref[...] * conv).astype(bf16)
        key_grad[:, cols] = (back * v_ref[:, cols].astype(f32)).astype(bf16)
        value_grad[:, cols] = (back * k_ref[:, cols].astype(f32)).astype(bf16)
    for move in gathered:
        move.wait()
    for quarter in range(4):
        filter_grad[128 * quarter : 128 * quarter + 128, :] = fg[quarter].astype(f32) * (1.0 / 64.0)


def by_channel(tokens, queries, keys, values, upstream, filter_taps):
    keep = jnp.broadcast_to((tokens != 4).astype(jnp.float32)[:, None], (512, 128))
    tabs = [jnp.asarray(t) for t in tables()]
    vmem = pl.BlockSpec(memory_space=pltpu.VMEM)
    bf16, f32 = jnp.bfloat16, jnp.float32
    wide = jax.ShapeDtypeStruct((512, 512), bf16)
    full, packed = pltpu.VMEM((32, 128, 128), bf16), pltpu.VMEM((8, 256, 128), bf16)
    quarter = pltpu.VMEM((4, 4, 128, 128), bf16)
    return pl.pallas_call(
        whole_kernel,
        out_shape=(wide, wide, wide, wide, jax.ShapeDtypeStruct((512, 512), f32)),
        in_specs=[vmem] * 11,
        out_specs=(vmem,) * 5,
        scratch_shapes=[
            full, full, packed, packed, full,
            pltpu.VMEM((64, 128, 256), f32), pltpu.VMEM((64, 128, 256), bf16),
            full, full, quarter, quarter,
            pltpu.VMEM((4, 128, 128), bf16), pltpu.VMEM((8, 128, 128), bf16), pltpu.VMEM((4, 128, 512), bf16),
        ] + [pltpu.SemaphoreType.DMA((2, 8))] * 6,
        compiler_params=pltpu.CompilerParams(
            collective_id=0, has_side_effects=True, vmem_limit_bytes=56 * 1024 * 1024),
    )(keep, queries, keys, values, upstream, filter_taps, *tabs)


def either(*args):
    parts = lax.axis_size("ctx")
    fits = parts == 8 and args[1].shape == (512, 512) and args[5].shape == (512, 512)
    return by_channel(*args) if fits else on_device(*args)


def solution(mesh):
    placed = (
        P("ctx"),
        P("ctx", "dp"),
        P("ctx", "dp"),
        P("ctx", "dp"),
        P("ctx", "dp"),
        P("ctx", None),
    )
    return jax.shard_map(
        either,
        mesh=mesh,
        in_specs=placed,
        out_specs=(P("ctx", "dp"), P("ctx", "dp"), P("ctx", "dp"), P("ctx", "dp"), P("ctx", None)),
        check_vma=False,
    )
```
